256 devices in a mesh: expert: 32 (over z, x), dp: 8 (over y, core).
Axes of the slice: x: 4, y: 4, z: 8, core: 2. Of those that a mesh axis runs over, the one named last changes fastest.
Arguments:
- tokens: bfloat16 [4096, 4096], P('expert', 'dp'), may hold values from -6 to 6
- out_grad: bfloat16 [4096, 4096], P('expert', 'dp'), may hold values from -6 to 6
- routes: int32 [4096, 4], P('expert'), may hold values from 0 to 31, all different within a row; in each aligned block of 128 rows (0 to 127, 128 to 255, ...) at most 18 rows name the same one
- gate_weights: float32 [4096, 4], P('expert'), may hold values from 0.05 to 0.5
- previous_home: int32 [32], replicated, may hold values from 0 to 31, each once
- next_home: int32 [32], replicated, may hold values from 0 to 31, each once
- w_in: bfloat16 [32, 2, 4096, 1024], P('expert', None, None, 'dp'), may hold values from -0.09375 to 0.09375
- w_out: bfloat16 [32, 1024, 4096], P('expert', 'dp'), may hold values from -0.1875 to 0.1875
- first_moment: float32 [32, 1024, 4096], P('expert', 'dp'), may hold values from -12 to 12
- second_moment: float32 [32, 1024, 4096], P('expert', 'dp'), may hold values from 1 to 30
Outputs:
- token_grad: bfloat16 [4096, 4096], P('expert', 'dp')
- new_first: float32 [32, 1024, 4096], P('expert', 'dp')
- new_second: float32 [32, 1024, 4096], P('expert', 'dp')
- adam_step: bfloat16 [32, 1024, 4096], P('expert', 'dp')
The draws below stay inside these ranges and needn't reach their ends.
Inputs may be any that keep to these rules, and one draw needn't show every extreme that they name: `routes`: in each device's block of 128 tokens at most 18 pairs name the same expert, and some block reaches 18. `previous_home`: each expert appears once. `next_home`: each expert appears once.
All inputs are finite; a program needn't handle non-finite values.
Results may differ from the reference program's by a relative error of at most 0.0064.
Values may be sent and summed in bfloat16 or wider, within the bound.
A program may use at most 128 MiB of HBM per device.

```python
import math
import jax
import jax.numpy as jnp
import numpy as np
from jax import lax

D = 4096
FF = 1024
TOP = 4
TOK_DEV = 128
EXPERTS = 32
HID = 128
CAP = 18
TOKENS = 4096
N_EXPERT = 32
N_DP = 8


def level_of(stream_key, shape, pieces, least, largest):
    def one(dim, shards_of):
        heights = jax.random.uniform(jax.random.fold_in(jax.random.fold_in(stream_key, 6), dim), (shards_of,), jnp.float32, least / len(pieces), largest / len(pieces))
        return jnp.repeat(jnp.exp(heights), shape[dim] // shards_of).reshape((-1,) + (1,) * (len(shape) - dim - 1))

    loudness = one(*pieces[0])
    for cut in pieces[1:]:
        loudness = loudness * one(*cut)
    return loudness


def deal_out(own_key, own, number, rows, count, top, limit, slope):
    sequence = jax.random.permutation(own_key, count)
    heavy_load, ordinary = portions_of(count, rows * top, limit, slope, True), portions_of(count, rows * top, limit, slope, False)
    places = jnp.arange(count)

    def named(tallies, offset_by):
        used = int((tallies > 0).sum())
        fixed = max(1, used // 4)
        shifted = fixed + (places - fixed + offset_by * (used - fixed)) % max(1, count - fixed)
        return jnp.zeros((count,), jnp.int32).at[sequence[jnp.where(places < fixed, places, shifted)]].set(jnp.asarray(tallies, jnp.int32))

    tallies = jnp.where(number % 4 == 0, named(heavy_load, number // 4), named(ordinary, number - number // 4 - 1))
    mixed = jax.random.permutation(jax.random.fold_in(own, 3), count)
    source_of, taker = mixed[0:count // 2 * 2:2], mixed[1:count // 2 * 2:2]
    room = jnp.minimum(tallies[source_of] - 1, limit - tallies[taker]) // 2
    room = jnp.where((source_of == sequence[0]) | (taker == sequence[0]) | (tallies[taker] == 0), 0, jnp.maximum(room, 0))
    shifted = jax.random.randint(jax.random.fold_in(own, 4), (count // 2,), 0, 1 << 20) % (room + 1)
    tallies = tallies.at[source_of].add(-shifted).at[taker].add(shifted)
    members = jnp.searchsorted(jnp.cumsum(tallies), jnp.arange(rows * top), side="right").astype(jnp.int32)
    table = members.reshape(top, rows).T
    table = table[jax.random.permutation(jax.random.fold_in(own, 1), rows)]
    offset_by = jax.random.randint(jax.random.fold_in(own, 2), (rows, 1), 0, top)
    return jnp.take_along_axis(table, (jnp.arange(top)[None, :] + offset_by) % top, axis=1)


def portions_of(amount, total, most, lean, full):
    loads = [(1 << 20) // math.isqrt(grade ** lean) + 1 for grade in range(1, amount + 1)]
    largest = most if full else min(most, max(-(-total // amount), total * loads[0] // sum(loads)))
    least = 1 if total - largest >= amount - 1 else 0
    given, spare = [largest] + [least] * (amount - 1), total - largest - least * (amount - 1)
    while spare > 0:
        movable = [i for i in range(1, amount) if given[i] < largest] or [i for i in range(1, amount) if given[i] < most]
        whole, budget = sum([loads[i] for i in movable]), spare
        for i in movable:
            addition = min(most - given[i], max(1, budget * loads[i] // whole), spare)
            given[i] = given[i] + addition
            spare = spare - addition
    return np.array(given)


def normal_values(rng, shape, deviation, reach, pieces=(), held_as=jnp.bfloat16):
    values = jax.random.normal(rng, shape, jnp.float32) * deviation
    if len(pieces) > 0:
        values = level_of(rng, shape, pieces, -0.22, 0.18) * values
    return jnp.clip(values, min=-reach, max=reach).astype(held_as)


def setup_inputs(seed: int = 0) -> dict:
    arg_keys = jax.random.split(jax.random.key(seed), 11)
    tokens = normal_values(arg_keys[0], (TOKENS, D), 1.0, 6.0, ((0, 32), (1, 8)))
    out_grad = normal_values(arg_keys[1], (TOKENS, D), 1.0, 6.0, ((0, 32), (1, 8)))
    routes_keys = jax.random.split(jax.random.fold_in(arg_keys[2], 1), TOKENS // TOK_DEV)
    routes_turns = jax.random.permutation(jax.random.fold_in(arg_keys[2], 3), TOKENS // TOK_DEV)
    routes = jax.vmap(lambda own, number: deal_out(jax.random.fold_in(arg_keys[2], 2), own, number, TOK_DEV, EXPERTS, TOP, CAP, 2))(routes_keys, routes_turns).reshape((TOKENS, TOP))
    gate_weights = jnp.clip(jnp.exp(math.log(0.5) - 2.3025851 * jax.random.uniform(arg_keys[3], (TOKENS, TOP), jnp.float32) ** level_of(arg_keys[3], (TOKENS, TOP), ((0, 32),), -0.2, 0.2)), 0.05, 0.5)
    previous_home = jax.random.permutation(arg_keys[4], EXPERTS).astype(jnp.int32)
    next_home = jax.random.permutation(arg_keys[5], EXPERTS).astype(jnp.int32)
    w_in = normal_values(arg_keys[6], (EXPERTS, 2, D, FF), D ** -0.5, 0.09375, ((0, 32), (3, 8)))
    w_out = normal_values(arg_keys[7], (EXPERTS, FF, D), FF ** -0.5, 0.1875, ((0, 32), (1, 8)))
    first_moment = normal_values(arg_keys[8], (EXPERTS, FF, D), 2.0, 12.0, ((0, 32), (1, 8)), jnp.float32)
    second_moment = jnp.clip(jnp.exp(math.log(30.0) - 3.4011974 * jax.random.uniform(arg_keys[9], (EXPERTS, FF, D), jnp.float32) ** level_of(arg_keys[9], (EXPERTS, FF, D), ((0, 32), (1, 8)), -0.2, 0.2)), 1.0, 30.0)
    return dict(tokens=tokens, out_grad=out_grad, routes=routes, gate_weights=gate_weights, previous_home=previous_home, next_home=next_home, w_in=w_in, w_out=w_out, first_moment=first_moment, second_moment=second_moment)


beta_one = 0.9
beta_two = 0.95
epsilon = 1e-08

def reference(tokens, out_grad, routes, gate_weights, previous_home, next_home, w_in, w_out, first_moment, second_moment):
    pairs = TOKENS * TOP
    onehot = (routes[:, :, None] == jnp.arange(EXPERTS, dtype=jnp.int32)[None, None, :]).astype(jnp.int32)
    onehot = onehot.reshape(N_EXPERT, TOK_DEV * TOP, EXPERTS)
    before = jnp.cumsum(onehot, axis=1) - onehot
    slot_index = lax.optimization_barrier(jnp.sum(before * onehot, axis=2))
    position = jnp.arange(N_EXPERT, dtype=jnp.int32)[:, None] * CAP + slot_index
    pair_table = jnp.full((EXPERTS, N_EXPERT * CAP), pairs, jnp.int32)
    pair_table = pair_table.at[routes.reshape(-1), position.reshape(-1)].set(jnp.arange(pairs, dtype=jnp.int32))
    zero_row = jnp.zeros((1, D), jnp.bfloat16)
    pair_rows = jnp.concatenate([jnp.repeat(tokens, TOP, axis=0), zero_row], axis=0)
    scaled = gate_weights.reshape(-1, 1) * jnp.repeat(out_grad, TOP, axis=0).astype(jnp.float32)
    pair_grads = jnp.concatenate([scaled.astype(jnp.bfloat16), zero_row], axis=0)

    def per_expert(expert):
        chosen = pair_table[expert]
        slot_rows = pair_rows[chosen]
        slot_grads = pair_grads[chosen]
        old_home = previous_home[expert]
        weight_in = w_in[old_home]
        weight_out = w_out[old_home]
        gate_pre = jnp.dot(slot_rows, weight_in[0], preferred_element_type=jnp.float32)
        up_value = jnp.dot(slot_rows, weight_in[1], preferred_element_type=jnp.float32)
        sigmoid_gate = jax.nn.sigmoid(gate_pre)
        silu_gate = gate_pre * sigmoid_gate
        activation = (silu_gate * up_value).astype(jnp.bfloat16)
        weight_grad = jnp.dot(activation.T, slot_grads, preferred_element_type=jnp.float32)
        act_grad = jnp.dot(slot_grads, weight_out.T, preferred_element_type=jnp.float32)
        gate_grad = (act_grad * up_value * sigmoid_gate * (1.0 + gate_pre * (1.0 - sigmoid_gate))).astype(jnp.bfloat16)
        up_grad = (act_grad * silu_gate).astype(jnp.bfloat16)
        summed = jnp.zeros((N_EXPERT * CAP, D), jnp.float32)
        for group_index in range(N_DP):
            lower_edge = group_index * HID
            upper_edge = lower_edge + HID
            partial_value = jnp.dot(gate_grad[:, lower_edge:upper_edge], weight_in[0][:, lower_edge:upper_edge].T, preferred_element_type=jnp.float32)
            partial_value = partial_value + jnp.dot(up_grad[:, lower_edge:upper_edge], weight_in[1][:, lower_edge:upper_edge].T, preferred_element_type=jnp.float32)
            partial_value = lax.optimization_barrier(partial_value.astype(jnp.bfloat16))
            summed = summed + partial_value.astype(jnp.float32)
        moment_one = beta_one * first_moment[old_home] + (1.0 - beta_one) * weight_grad
        moment_two = beta_two * second_moment[old_home] + (1.0 - beta_two) * weight_grad * weight_grad
        step_value = (moment_one / (jnp.sqrt(moment_two) + epsilon)).astype(jnp.bfloat16)
        return (moment_one, moment_two, step_value, summed)
    moment_one, moment_two, step_value, slot_sums = lax.map(per_expert, jnp.arange(EXPERTS, dtype=jnp.int32))
    pair_sum = jnp.zeros((pairs + 1, D), jnp.float32).at[pair_table.reshape(-1)].add(slot_sums.reshape(-1, D))
    token_grad = pair_sum[:pairs].reshape(TOKENS, TOP, D).sum(axis=1).astype(jnp.bfloat16)
    new_first = jnp.zeros_like(moment_one).at[next_home].set(moment_one)
    new_second = jnp.zeros_like(moment_two).at[next_home].set(moment_two)
    adam_step = jnp.zeros_like(step_value).at[next_home].set(step_value)
    return (token_grad, new_first, new_second, adam_step)
```

```python
import jax
import jax.numpy as jnp
from jax import lax
from jax.sharding import PartitionSpec as P

beta_one = 0.9
beta_two = 0.95
epsilon = 1e-08


def per_device(
    tokens,
    out_grad,
    routes,
    gate_weights,
    previous_home,
    next_home,
    w_in,
    w_out,
    first_moment,
    second_moment,
):
    devices = lax.axis_size("expert")
    parts = lax.axis_size("dp")
    tok_count, top_count = routes.shape
    experts = previous_home.shape[0]
    capacity = tok_count * top_count * 9 // (8 * experts)
    slot_total = devices * capacity
    width = w_out.shape[2]
    hidden = w_out.shape[1]
    local = tokens.shape[1]
    piece = width // devices
    pairs = tok_count * top_count

    def across(values):
        return lax.all_to_all(values, "expert", split_axis=0, concat_axis=0, tiled=True)

    device_index = jnp.arange(devices, dtype=jnp.int32)
    matched = (next_home[:, None] == device_index[None, :]).astype(jnp.int32)
    source = jnp.sum(matched * previous_home[:, None], axis=0)

    both = jnp.stack([first_moment[0], second_moment[0]]).astype(jnp.bfloat16)
    both = both.reshape(2, hidden, devices, piece).transpose(2, 0, 1, 3)
    spread = across(both)

    flat = routes.reshape(pairs)
    onehot = flat[:, None] == jnp.arange(experts, dtype=jnp.int32)[None, :]
    order = jnp.arange(pairs, dtype=jnp.int32)
    lower = (order[None, :] < order[:, None]).astype(jnp.bfloat16)
    before = jnp.dot(lower, onehot.astype(jnp.bfloat16), preferred_element_type=jnp.float32)
    slot_index = jnp.sum(jnp.where(onehot, before, 0.0), axis=1).astype(jnp.int32)
    target = jnp.sum(jnp.where(onehot, previous_home[None, :], 0), axis=1)
    position = (target * capacity + slot_index).reshape(tok_count, top_count)
    hit = position[None] == jnp.arange(slot_total, dtype=jnp.int32)[:, None, None]
    place = jnp.any(hit, axis=2).astype(jnp.bfloat16)
    gate_of = jnp.sum(jnp.where(hit, gate_weights[None], 0.0), axis=(1, 2))

    send_rows = jnp.dot(place, tokens, preferred_element_type=jnp.float32)
    send_grads = jnp.dot(place, out_grad, preferred_element_type=jnp.float32) * gate_of[:, None]
    send = jnp.concatenate([send_rows, send_grads], axis=1).astype(jnp.bfloat16)
    here = across(send.reshape(devices, capacity, 2 * local)).reshape(slot_total, 2 * local)
    full = lax.all_gather(here, "dp", axis=0, tiled=False)

    def side(start):
        return full[:, :, start : start + local].transpose(1, 0, 2).reshape(slot_total, width)

    slot_rows, slot_grads = side(0), side(local)
    gate_in, up_in, out_rows = w_in[0, 0], w_in[0, 1], w_out[0]
    gate_pre = jnp.dot(slot_rows, gate_in, preferred_element_type=jnp.float32)
    up_value = jnp.dot(slot_rows, up_in, preferred_element_type=jnp.float32)
    sigmoid_gate = jax.nn.sigmoid(gate_pre)
    silu_gate = gate_pre * sigmoid_gate
    activation = (silu_gate * up_value).astype(jnp.bfloat16)
    over_columns = (((1,), (1,)), ((), ()))
    weight_grad = lax.dot_general(
        activation, slot_grads, (((0,), (0,)), ((), ())), preferred_element_type=jnp.float32
    )
    wg_spread = across(
        weight_grad.astype(jnp.bfloat16).reshape(hidden, devices, piece).transpose(1, 0, 2)
    )
    act_grad = lax.dot_general(
        slot_grads, out_rows, over_columns, preferred_element_type=jnp.float32
    )
    gate_grad = (
        act_grad * up_value * sigmoid_gate * (1.0 + gate_pre * (1.0 - sigmoid_gate))
    ).astype(jnp.bfloat16)
    up_grad = (act_grad * silu_gate).astype(jnp.bfloat16)
    partial_value = lax.dot_general(
        gate_grad, gate_in, over_columns, preferred_element_type=jnp.float32
    ) + lax.dot_general(up_grad, up_in, over_columns, preferred_element_type=jnp.float32)
    pieces = partial_value.astype(jnp.bfloat16).reshape(slot_total, parts, local).transpose(1, 0, 2)
    pieces = lax.all_to_all(pieces, "dp", split_axis=0, concat_axis=0, tiled=True)
    summed = jnp.sum(pieces.astype(jnp.float32), axis=0).astype(jnp.bfloat16)
    returned = across(summed.reshape(devices, capacity, local)).reshape(slot_total, local)
    token_grad = lax.dot_general(
        place, returned, (((0,), (0,)), ((), ())), preferred_element_type=jnp.float32
    ).astype(jnp.bfloat16)

    pick = (source[:, None] == device_index[None, :]).astype(jnp.bfloat16)
    held = jnp.tensordot(pick, spread, 1, preferred_element_type=jnp.float32)
    grad_piece = jnp.tensordot(pick, wg_spread, 1, preferred_element_type=jnp.float32)
    mid_first = beta_one * held[:, 0] + (1.0 - beta_one) * grad_piece
    mid_second = beta_two * held[:, 1] + (1.0 - beta_two) * grad_piece * grad_piece
    back = across(jnp.stack([mid_first, mid_second], axis=1).astype(jnp.bfloat16))
    back = back.transpose(1, 2, 0, 3).reshape(2, 1, hidden, width).astype(jnp.float32)
    new_first, new_second = back[0], back[1]
    adam_step = (new_first / (jnp.sqrt(new_second) + epsilon)).astype(jnp.bfloat16)
    return (token_grad, new_first, new_second, adam_step)


def solution(mesh):
    return jax.shard_map(
        per_device,
        mesh=mesh,
        in_specs=(
            P("expert", "dp"),
            P("expert", "dp"),
            P("expert", None),
            P("expert", None),
            P(),
            P(),
            P("expert", None, None, "dp"),
            P("expert", "dp", None),
            P("expert", "dp", None),
            P("expert", "dp", None),
        ),
        out_specs=(
            P("expert", "dp"),
            P("expert", "dp", None),
            P("expert", "dp", None),
            P("expert", "dp", None),
        ),
        check_vma=False,
    )
```

```python
import functools

import jax
import jax.numpy as jnp
from jax import lax
from jax.experimental import pallas as pl
from jax.experimental.pallas import tpu as pltpu
from jax.sharding import PartitionSpec as P

beta_one = 0.9
beta_two = 0.95
epsilon = 1e-08

NE = 32
NZ, NX = 8, 4
ND = 8
NY = 4
TOK = 128
TOP = 4
MAIN = 16
OVER = 2
LANE = 128
FEAT = 512
WIDTH = 4096
HID = 128
ROWS = NE * MAIN
EXTRA = NE * OVER
SLOTS = ROWS + EXTRA
PACK = 2 * FEAT + LANE
BACK = FEAT + LANE
BLOCK = NX * MAIN
F32 = jnp.float32
BF16 = jnp.bfloat16
MESH = pl.DeviceIdType.MESH
VMEM_LIMIT = 60 << 20


def iota(shape, dim):
    return lax.broadcasted_iota(jnp.int32, shape, dim)


def dot(a, b, dims=((1,), (0,))):
    return lax.dot_general(a, b, (dims, ((), ())), preferred_element_type=F32)


def prepare_kernel(
    home_ref, routes_ref, gates_ref, tok_ref, grad_ref, send_ref, main_ref, over_ref, code_x, gate_x
):
    routes = routes_ref[...]
    target = jnp.zeros_like(routes)
    for e in range(NE):
        target = jnp.where(routes == e, home_ref[e], target)
    dest = iota((NE, TOK), 0)
    chosen = jnp.zeros((NE, TOK), F32)
    gate = jnp.zeros((NE, TOK), F32)
    for k in range(TOP):
        same = target[k : k + 1, :] == dest
        chosen = jnp.where(same, 1.0, chosen)
        gate = jnp.where(same, gates_ref[k : k + 1, :], gate)
    earlier = jnp.where(iota((TOK, TOK), 0) < iota((TOK, TOK), 1), 1.0, 0.0).astype(BF16)
    count = dot(chosen.astype(BF16), earlier)
    code = jnp.where(chosen > 0.5, count, -1.0)
    for j in range(NE):
        rows = pl.ds(j * MAIN, MAIN)
        code_x[rows, :] = jnp.broadcast_to(code[j : j + 1, :], (MAIN, TOK))
        gate_x[rows, :] = jnp.broadcast_to(gate[j : j + 1, :], (MAIN, TOK))
    code = code_x[...]
    gate = gate_x[...]
    within = iota((ROWS, TOK), 0) % MAIN
    hit = code == within.astype(F32)
    place = jnp.where(hit, 1.0, 0.0).astype(BF16)
    scale = jnp.sum(jnp.where(hit, gate, 0.0), axis=1, keepdims=True)
    main_ref[...] = place
    send_ref[:, 0:FEAT] = dot(place, tok_ref[...]).astype(BF16)
    send_ref[:, FEAT : 2 * FEAT] = (dot(place, grad_ref[...]) * scale).astype(BF16)
    hit = code == (MAIN + within % OVER).astype(F32)
    scale = jnp.sum(jnp.where(hit, gate, 0.0), axis=1, keepdims=True)
    over_ref[...] = jnp.where(hit, 1.0, 0.0).astype(BF16)
    chunk = within // OVER
    packed = jnp.zeros((ROWS, LANE), F32)
    for c in range(8):
        part = jnp.where(hit & (chunk == c), 1.0, 0.0).astype(BF16)
        held = tok_ref if c < 4 else grad_ref
        packed = packed + dot(part, held[:, (c % 4) * LANE : (c % 4 + 1) * LANE])
    packed = jnp.where(chunk >= 4, packed * scale, packed)
    send_ref[:, 2 * FEAT : PACK] = packed.astype(BF16)


def main_kernel(
    source_ref,
    send_ref,
    first_hbm,
    second_hbm,
    win_hbm,
    wout_hbm,
    ret_ref,
    back_ref,
    g,
    first_v,
    second_v,
    wgu,
    wout,
    raw_s,
    raw_r,
    wg_s,
    wg_r,
    back_s,
    u,
    sib_r,
    pair,
    y_r,
    xt,
    xg,
    acc,
    agrad,
    act,
    act_t,
    gu,
    ret_s,
    sel,
    load_sem,
    own_sem,
    disp_ss,
    disp_rs,
    raw_ss,
    raw_rs,
    wg_ss,
    wg_rs,
    back_ss,
    back_rs,
    ret_ss,
    ret_rs,
    near_ss,
    near_rs,
    sib_ss,
    sib_rs,
    sum_ss,
    sum_rs,
    ysum_ss,
    ysum_rs,
):
    e = lax.axis_index("expert")
    d = lax.axis_index("dp")
    z, x = lax.div(e, NX), lax.rem(e, NX)
    y, c = lax.div(d, 2), lax.rem(d, 2)
    sib = y * 2 + 1 - c

    def dz_of(i):
        odd = i % 2
        return odd * ((i + 1) // 2) + (1 - odd) * ((NZ - i // 2) % NZ)

    def target(k):
        i, dx = lax.div(k, NX), lax.rem(k, NX)
        odd = lax.rem(i, 2)
        dz = odd * lax.div(i + 1, 2) + (1 - odd) * lax.rem(NZ - lax.div(i, 2), NZ)
        return lax.rem(z + dz, NZ) * NX + lax.rem(x + dx, NX)

    def y_of(step):
        return lax.rem(y + step + NY, NY) * 2 + c

    def loop(body, lower=1, upper=NE):
        def step(k, carry):
            body(k)
            return carry

        lax.fori_loop(lower, upper, step, 0)

    barrier = pltpu.get_barrier_semaphore()

    def greet(k):
        pl.semaphore_signal(barrier, inc=1, device_id=(target(k), d), device_id_type=MESH)

    loop(greet)
    for peer in (y_of(1), y_of(2), y_of(3), sib):
        pl.semaphore_signal(barrier, inc=1, device_id=(e, peer), device_id_type=MESH)

    loads = [
        pltpu.make_async_copy(first_hbm.at[0], first_v, load_sem.at[0]),
        pltpu.make_async_copy(second_hbm.at[0], second_v, load_sem.at[1]),
        pltpu.make_async_copy(win_hbm.at[0, 0], wgu.at[:, pl.ds(0, HID)], load_sem.at[2]),
        pltpu.make_async_copy(win_hbm.at[0, 1], wgu.at[:, pl.ds(HID, HID)], load_sem.at[3]),
        pltpu.make_async_copy(wout_hbm.at[0], wout, load_sem.at[4]),
    ]
    for load in loads:
        load.start()
    pl.semaphore_wait(barrier, NE - 1 + 4)

    def rows16(j):
        return pl.ds(pl.multiple_of(j * MAIN, MAIN), MAIN)

    def remote(src, dst, ss, rs, who):
        return pltpu.make_async_remote_copy(
            src_ref=src, dst_ref=dst, send_sem=ss, recv_sem=rs, device_id=who, device_id_type=MESH
        )

    def disp(k):
        to = target(k)
        return remote(
            send_ref.at[rows16(to)], g.at[d, rows16(e)], disp_ss.at[k], disp_rs.at[k], (to, d)
        )

    def raw(k):
        to = target(k)
        return remote(raw_s.at[to], raw_r.at[e], raw_ss.at[k], raw_rs.at[k], (to, d))

    def wg(k):
        to = target(k)
        return remote(wg_s.at[to], wg_r.at[e], wg_ss.at[k], wg_rs.at[k], (to, d))

    def back(k):
        to = target(k)
        return remote(back_s.at[to], back_ref.at[e], back_ss.at[k], back_rs.at[k], (to, d))

    def ret(k):
        to = target(k)
        return remote(
            ret_s.at[rows16(to)], ret_ref.at[rows16(e)], ret_ss.at[k], ret_rs.at[k], (to, d)
        )

    loop(lambda k: disp(k).start())
    own = [
        pltpu.make_async_copy(send_ref.at[rows16(e)], g.at[d, rows16(e)], own_sem.at[0]),
        pltpu.make_async_copy(raw_s.at[e], raw_r.at[e], own_sem.at[1]),
        pltpu.make_async_copy(wg_s.at[e], wg_r.at[e], own_sem.at[2]),
        pltpu.make_async_copy(back_s.at[e], back_ref.at[e], own_sem.at[3]),
        pltpu.make_async_copy(ret_s.at[rows16(e)], ret_ref.at[rows16(e)], own_sem.at[4]),
    ]
    own[0].start()

    loads[0].wait()
    loads[1].wait()

    def cut(j):
        cols = pl.ds(pl.multiple_of(j * LANE, LANE), LANE)
        raw_s[j, 0] = first_v[:, cols].astype(BF16)
        raw_s[j, 1] = second_v[:, cols].astype(BF16)

    loop(cut, 0)
    r, q = iota((ROWS, ROWS), 0), iota((ROWS, ROWS), 1)
    spot = (r % EXTRA) // OVER * MAIN + r // EXTRA * OVER + r % OVER
    sel[...] = jnp.where(q == spot, 1.0, 0.0).astype(BF16)

    def block(i):
        return pl.ds(pl.multiple_of(lax.rem(z + NZ - dz_of(i), NZ) * BLOCK, BLOCK), BLOCK)

    def near(way, hop, i):
        step = 1 if way == 0 else -1
        held = g.at[y_of(-step * hop), block(i)]
        n = (way * 2 + hop) * NZ + i
        return remote(held, held, near_ss.at[n], near_rs.at[n], (e, y_of(step)))

    def side(back_by, i):
        held = g.at[y_of(-back_by), block(i)]
        n = (back_by % NY) * NZ + i
        return remote(held, held, sib_ss.at[n], sib_rs.at[n], (e, sib))

    def from_near(i):
        near(0, 0, i).wait_recv()
        if i % 2 == 0:
            near(0, 1, i).start()
        side(1, i).start()
        near(1, 0, i).wait_recv()
        if i % 2 == 1:
            near(1, 1, i).start()
        side(3, i).start()

    def from_far(i):
        near(i % 2, 1, i).wait_recv()
        side(2, i).start()

    for i in range(NZ):
        for dx in range(NX):
            if i == 0 and dx == 0:
                own[0].wait()
            else:
                disp(jnp.int32(i * NX + dx)).wait_recv()
        near(0, 0, i).start()
        near(1, 0, i).start()
        side(0, i).start()
        if i >= 1:
            from_near(i - 1)
        if i >= 2:
            from_far(i - 2)
    loop(lambda k: raw(k).start())
    own[1].start()
    from_near(NZ - 1)
    from_far(NZ - 2)
    from_far(NZ - 1)
    for load in loads[2:]:
        load.wait()
    for i in range(NZ):
        for b in range(NY):
            side(b, i).wait_recv()

    def part(j):
        return pl.ds(pl.multiple_of(j * FEAT, FEAT), FEAT)

    def lanes(j):
        return pl.ds(pl.multiple_of(j * LANE, LANE), LANE)

    def unpack(j):
        moved = dot(sel[...], g[j, :, 2 * FEAT : PACK]).astype(BF16)
        for k in range(4):
            xt[:, lanes(j * 4 + k)] = moved[k * EXTRA : (k + 1) * EXTRA]
            xg[:, lanes(j * 4 + k)] = moved[(k + 4) * EXTRA : (k + 5) * EXTRA]

    loop(unpack, 0, ND)
    acc[...] = jnp.zeros_like(acc)
    agrad[...] = jnp.zeros_like(agrad)

    def forward(j):
        w = wgu[part(j), :]
        acc[0:ROWS] += dot(g[j, :, 0:FEAT], w)
        acc[ROWS:SLOTS] += dot(xt[:, part(j)], w)
        o = wout[:, part(j)]
        agrad[0:ROWS] += dot(g[j, :, FEAT : 2 * FEAT], o, ((1,), (1,)))
        agrad[ROWS:SLOTS] += dot(xg[:, part(j)], o, ((1,), (1,)))

    loop(forward, 0, ND)

    def pointwise(j):
        rows = pl.ds(pl.multiple_of(j * EXTRA, EXTRA), EXTRA)
        gate, up, ag = acc[rows, 0:HID], acc[rows, HID : 2 * HID], agrad[rows]
        sig = jax.nn.sigmoid(gate)
        silu = gate * sig
        act[rows] = silu * up
        gu[rows, 0:HID] = (ag * up * sig * (1.0 + gate * (1.0 - sig))).astype(BF16)
        gu[rows, HID : 2 * HID] = (ag * silu).astype(BF16)

    loop(pointwise, 0, SLOTS // EXTRA)
    act_t[...] = act[...].T.astype(BF16)

    def outer(j):
        w = dot(act_t[:, 0:ROWS], g[j, :, FEAT : 2 * FEAT])
        w = w + dot(act_t[:, ROWS:SLOTS], xg[:, part(j)])
        for k in range(4):
            wg_s[j * 4 + k] = w[:, k * LANE : (k + 1) * LANE].astype(BF16)

    loop(outer, 0, ND)
    loop(lambda k: wg(k).start())
    own[2].start()

    def share(j):
        u[j] = dot(gu[...], wgu[part(j), :], ((1,), (1,))).astype(BF16)

    def to_sib(j):
        return remote(u.at[j * 2 + 1 - c], sib_r.at[j], sum_ss.at[j], sum_rs.at[j], (e, sib))

    def shares_out(j):
        share(j * 2 + 1 - c)
        to_sib(j).start()

    loop(shares_out, 0, NY)
    loop(lambda j: share(j * 2 + c), 0, NY)

    def to_y(o):
        return remote(
            pair.at[o], y_r.at[o], ysum_ss.at[o], ysum_rs.at[o], (e, lax.rem(y + o, NY) * 2 + c)
        )

    loop(lambda j: to_sib(j).wait_recv(), 0, NY)
    for o in (1, 3, 2, 0):
        ty = lax.rem(y + o, NY)
        pair[o] = (u[ty * 2 + c].astype(F32) + sib_r[ty].astype(F32)).astype(BF16)
        if o:
            to_y(o).start()

    own[1].wait()
    own[2].wait()
    loop(lambda k: raw(k).wait_recv())
    loop(lambda k: wg(k).wait_recv())

    def update(to):
        j = source_ref[to]
        w = wg_r[j].astype(F32)
        back_s[to, 0] = (beta_one * raw_r[j, 0].astype(F32) + (1.0 - beta_one) * w).astype(BF16)
        back_s[to, 1] = (
            beta_two * raw_r[j, 1].astype(F32) + (1.0 - beta_two) * w * w
        ).astype(BF16)

    def send_back(k):
        update(target(k))
        back(k).start()

    loop(send_back)
    update(e)
    own[3].start()

    for o in (1, 3, 2):
        to_y(o).wait_recv()

    def total(rows):
        value = pair[0, rows].astype(F32)
        for o in (1, 2, 3):
            value = value + y_r[o, rows].astype(F32)
        return value.astype(BF16)

    def add(j):
        rows = pl.ds(pl.multiple_of(j * EXTRA, EXTRA), EXTRA)
        ret_s[rows, 0:FEAT] = total(rows)

    loop(add, 0, ROWS // EXTRA)
    rest = total(pl.ds(ROWS, EXTRA))
    packed = jnp.zeros((ROWS, LANE), F32)
    for k in range(4):
        packed = packed + dot(
            sel[k * EXTRA : (k + 1) * EXTRA, :],
            rest[:, k * LANE : (k + 1) * LANE],
            ((0,), (0,)),
        )
    ret_s[:, FEAT:BACK] = packed.astype(BF16)
    loop(lambda k: ret(k).start())
    own[4].start()

    loop(lambda k: disp(k).wait_send())
    loop(lambda k: raw(k).wait_send())
    loop(lambda k: wg(k).wait_send())
    for i in range(NZ):
        near(0, 0, i).wait_send()
        near(1, 0, i).wait_send()
        near(i % 2, 1, i).wait_send()
        for b in range(NY):
            side(b, i).wait_send()
    loop(lambda j: to_sib(j).wait_send(), 0, NY)
    loop(lambda o: to_y(o).wait_send(), 1, NY)
    own[3].wait()
    loop(lambda k: back(k).wait())
    own[4].wait()
    loop(lambda k: ret(k).wait())


def finish_kernel(back_ref, ret_ref, main_ref, over_ref, tok_ref, first_ref, second_ref, step_ref):
    for k in range(4):
        cols = slice(k * LANE, (k + 1) * LANE)
        one, two = back_ref[k, 0].astype(F32), back_ref[k, 1].astype(F32)
        first_ref[0, :, cols] = one
        second_ref[0, :, cols] = two
        step_ref[0, :, cols] = (one / (jnp.sqrt(two) + epsilon)).astype(BF16)

    @pl.when(pl.program_id(0) == 0)
    def _():
        total = dot(main_ref[...], ret_ref[:, 0:FEAT], ((0,), (0,)))
        chunk = iota((ROWS, TOK), 0) % MAIN // OVER
        for k in range(4):
            cols = slice(k * LANE, (k + 1) * LANE)
            part = jnp.where(chunk == k, over_ref[...].astype(F32), 0.0).astype(BF16)
            more = dot(part, ret_ref[:, FEAT:BACK], ((0,), (0,)))
            tok_ref[:, cols] = (total[:, cols] + more).astype(BF16)


def per_device(
    tokens,
    out_grad,
    routes,
    gate_weights,
    previous_home,
    next_home,
    w_in,
    w_out,
    first_moment,
    second_moment,
):
    device_index = jnp.arange(NE, dtype=jnp.int32)
    matched = (next_home[:, None] == device_index[None, :]).astype(jnp.int32)
    source = jnp.sum(matched * previous_home[:, None], axis=0)

    vmem = pl.BlockSpec(memory_space=pltpu.VMEM)
    smem = pl.BlockSpec(memory_space=pltpu.SMEM)
    anywhere = pl.BlockSpec(memory_space=pl.ANY)
    shape = jax.ShapeDtypeStruct
    send, place_main, place_over = pl.pallas_call(
        prepare_kernel,
        out_shape=(
            shape((ROWS, PACK), BF16),
            shape((ROWS, TOK), BF16),
            shape((ROWS, TOK), BF16),
        ),
        in_specs=[smem, vmem, vmem, vmem, vmem],
        out_specs=(vmem, vmem, vmem),
        scratch_shapes=[pltpu.VMEM((ROWS, TOK), F32), pltpu.VMEM((ROWS, TOK), F32)],
        compiler_params=pltpu.CompilerParams(vmem_limit_bytes=32 << 20),
        cost_estimate=pl.CostEstimate(flops=3 * 10**8, bytes_accessed=2 << 20, transcendentals=0),
        name="prepare",
    )(previous_home, routes.T, gate_weights.T, tokens, out_grad)

    dma = pltpu.SemaphoreType.DMA
    ret, back = pl.pallas_call(
        main_kernel,
        out_shape=(shape((ROWS, BACK), BF16), shape((NE, 2, HID, LANE), BF16)),
        in_specs=[smem, vmem, anywhere, anywhere, anywhere, anywhere],
        out_specs=(vmem, vmem),
        scratch_shapes=[
            pltpu.VMEM((ND, ROWS, PACK), BF16),
            pltpu.VMEM((HID, WIDTH), F32),
            pltpu.VMEM((HID, WIDTH), F32),
            pltpu.VMEM((WIDTH, 2 * HID), BF16),
            pltpu.VMEM((HID, WIDTH), BF16),
            pltpu.VMEM((NE, 2, HID, LANE), BF16),
            pltpu.VMEM((NE, 2, HID, LANE), BF16),
            pltpu.VMEM((NE, HID, LANE), BF16),
            pltpu.VMEM((NE, HID, LANE), BF16),
            pltpu.VMEM((NE, 2, HID, LANE), BF16),
            pltpu.VMEM((ND, SLOTS, FEAT), BF16),
            pltpu.VMEM((NY, SLOTS, FEAT), BF16),
            pltpu.VMEM((NY, SLOTS, FEAT), BF16),
            pltpu.VMEM((NY, SLOTS, FEAT), BF16),
            pltpu.VMEM((EXTRA, WIDTH), BF16),
            pltpu.VMEM((EXTRA, WIDTH), BF16),
            pltpu.VMEM((SLOTS, 2 * HID), F32),
            pltpu.VMEM((SLOTS, HID), F32),
            pltpu.VMEM((SLOTS, HID), F32),
            pltpu.VMEM((HID, SLOTS), BF16),
            pltpu.VMEM((SLOTS, 2 * HID), BF16),
            pltpu.VMEM((ROWS, BACK), BF16),
            pltpu.VMEM((ROWS, ROWS), BF16),
            dma((5,)),
            dma((5,)),
        ]
        + [dma((NE,))] * 14
        + [dma((NY,))] * 4,
        compiler_params=pltpu.CompilerParams(
            collective_id=0, has_side_effects=True, vmem_limit_bytes=VMEM_LIMIT
        ),
        cost_estimate=pl.CostEstimate(
            flops=4 * 10**9, bytes_accessed=16 << 20, transcendentals=1 << 17
        ),
        name="exchange",
    )(source, send, first_moment, second_moment, w_in, w_out)

    steps = 8
    span = WIDTH // steps
    whole = lambda s: pl.BlockSpec(s, lambda i: (0,) * len(s))
    wide = pl.BlockSpec((1, HID, span), lambda i: (0, 0, i))
    return pl.pallas_call(
        finish_kernel,
        grid=(steps,),
        out_shape=(
            shape((TOK, FEAT), BF16),
            shape((1, HID, WIDTH), F32),
            shape((1, HID, WIDTH), F32),
            shape((1, HID, WIDTH), BF16),
        ),
        in_specs=[
            pl.BlockSpec((NE // steps, 2, HID, LANE), lambda i: (i, 0, 0, 0)),
            whole((ROWS, BACK)),
            whole((ROWS, TOK)),
            whole((ROWS, TOK)),
        ],
        out_specs=(whole((TOK, FEAT)), wide, wide, wide),
        compiler_params=pltpu.CompilerParams(vmem_limit_bytes=32 << 20),
        cost_estimate=pl.CostEstimate(
            flops=3 * 10**8, bytes_accessed=8 << 20, transcendentals=1 << 19
        ),
        name="finish",
    )(back, ret, place_main, place_over)


def solution(mesh):
    return jax.shard_map(
        per_device,
        mesh=mesh,
        in_specs=(
            P("expert", "dp"),
            P("expert", "dp"),
            P("expert", None),
            P("expert", None),
            P(),
            P(),
            P("expert", None, None, "dp"),
            P("expert", "dp", None),
            P("expert", "dp", None),
            P("expert", "dp", None),
        ),
        out_specs=(
            P("expert", "dp"),
            P("expert", "dp", None),
            P("expert", "dp", None),
            P("expert", "dp", None),
        ),
        check_vma=False,
    )
```

```python
import functools

import jax
import jax.numpy as jnp
from jax import lax
from jax.experimental import pallas as pl
from jax.experimental.pallas import tpu as pltpu
from jax.sharding import PartitionSpec as P

beta_one = 0.9
beta_two = 0.95
epsilon = 1e-08

NE = 32
NZ, NX = 8, 4
ND = 8
NY = 4
TOK = 128
TOP = 4
MAIN = 16
OVER = 2
LANE = 128
FEAT = 512
WIDTH = 4096
HID = 128
ROWS = NE * MAIN
EXTRA = NE * OVER
SLOTS = ROWS + EXTRA
PACK = 2 * FEAT + LANE
BACK = FEAT + LANE
BLOCK = NX * MAIN
RAW = 112
POST = 2 * HID - RAW
RAW_AT = 3
RAW_N = 8
LEAD = 5
F32 = jnp.float32
BF16 = jnp.bfloat16
MESH = pl.DeviceIdType.MESH
VMEM_LIMIT = 60 << 20


def iota(shape, dim):
    return lax.broadcasted_iota(jnp.int32, shape, dim)


def dot(a, b, dims=((1,), (0,))):
    return lax.dot_general(a, b, (dims, ((), ())), preferred_element_type=F32)


def prepare(
    home_ref, routes_ref, gates_ref, tok_ref, grad_ref, send_ref, main_ref, over_ref, code_x, gate_x
):
    routes = routes_ref[...]
    target = jnp.zeros_like(routes)
    for e in range(NE):
        target = jnp.where(routes == e, home_ref[e], target)
    dest = iota((NE, TOK), 0)
    chosen = jnp.zeros((NE, TOK), F32)
    gate = jnp.zeros((NE, TOK), F32)
    for k in range(TOP):
        same = target[k : k + 1, :] == dest
        chosen = jnp.where(same, 1.0, chosen)
        gate = jnp.where(same, gates_ref[k : k + 1, :], gate)
    earlier = jnp.where(iota((TOK, TOK), 0) < iota((TOK, TOK), 1), 1.0, 0.0).astype(BF16)
    count = dot(chosen.astype(BF16), earlier)
    code = jnp.where(chosen > 0.5, count, -1.0)
    for j in range(NE):
        rows = pl.ds(j * MAIN, MAIN)
        code_x[rows, :] = jnp.broadcast_to(code[j : j + 1, :], (MAIN, TOK))
        gate_x[rows, :] = jnp.broadcast_to(gate[j : j + 1, :], (MAIN, TOK))
    code = code_x[...]
    gate = gate_x[...]
    within = iota((ROWS, TOK), 0) % MAIN
    hit = code == within.astype(F32)
    place = jnp.where(hit, 1.0, 0.0).astype(BF16)
    scale = jnp.sum(jnp.where(hit, gate, 0.0), axis=1, keepdims=True)
    main_ref[...] = place
    send_ref[:, 0:FEAT] = dot(place, tok_ref[...]).astype(BF16)
    send_ref[:, FEAT : 2 * FEAT] = (dot(place, grad_ref[...]) * scale).astype(BF16)
    hit = code == (MAIN + within % OVER).astype(F32)
    scale = jnp.sum(jnp.where(hit, gate, 0.0), axis=1, keepdims=True)
    over_ref[...] = jnp.where(hit, 1.0, 0.0).astype(BF16)
    chunk = within // OVER
    packed = jnp.zeros((ROWS, LANE), F32)
    for c in range(8):
        part = jnp.where(hit & (chunk == c), 1.0, 0.0).astype(BF16)
        held = tok_ref if c < 4 else grad_ref
        packed = packed + dot(part, held[:, (c % 4) * LANE : (c % 4 + 1) * LANE])
    packed = jnp.where(chunk >= 4, packed * scale, packed)
    send_ref[:, 2 * FEAT : PACK] = packed.astype(BF16)


def main_kernel(
    previous_ref,
    next_ref,
    routes_hbm,
    gates_hbm,
    tok_hbm,
    grad_hbm,
    first_hbm,
    second_hbm,
    win_hbm,
    wout_hbm,
    ret_ref,
    back_ref,
    main_ref,
    over_ref,
    routes_v,
    gates_v,
    tok_v,
    grad_v,
    send_ref,
    code_x,
    gate_x,
    g,
    first_v,
    second_v,
    wgu,
    wout,
    raw_s,
    raw_r,
    wg_s,
    wg_r,
    back_s,
    u,
    sib_r,
    pair,
    y_r,
    xt,
    xg,
    acc,
    agrad,
    act,
    act_t,
    gu,
    ret_s,
    sel,
    load_sem,
    own_sem,
    disp_ss,
    disp_rs,
    raw_ss,
    raw_rs,
    wg_ss,
    wg_rs,
    back_ss,
    back_rs,
    ret_ss,
    ret_rs,
    near_ss,
    near_rs,
    sib_ss,
    sib_rs,
    sum_ss,
    sum_rs,
    ysum_ss,
    ysum_rs,
):
    e = lax.axis_index("expert")
    d = lax.axis_index("dp")
    z, x = lax.div(e, NX), lax.rem(e, NX)
    y, c = lax.div(d, 2), lax.rem(d, 2)
    sib = y * 2 + 1 - c

    def dz_of(i):
        odd = i % 2
        return odd * ((i + 1) // 2) + (1 - odd) * ((NZ - i // 2) % NZ)

    def target(k):
        i, dx = lax.div(k, NX), lax.rem(k, NX)
        odd = lax.rem(i, 2)
        dz = odd * lax.div(i + 1, 2) + (1 - odd) * lax.rem(NZ - lax.div(i, 2), NZ)
        return lax.rem(z + dz, NZ) * NX + lax.rem(x + dx, NX)

    def y_of(step):
        return lax.rem(y + step + NY, NY) * 2 + c

    def loop(body, lower=1, upper=NE):
        def step(k, carry):
            body(k)
            return carry

        lax.fori_loop(lower, upper, step, 0)

    barrier = pltpu.get_barrier_semaphore()

    def greet(k):
        pl.semaphore_signal(barrier, inc=1, device_id=(target(k), d), device_id_type=MESH)

    loop(greet)
    for peer in (y_of(1), y_of(2), y_of(3), sib):
        pl.semaphore_signal(barrier, inc=1, device_id=(e, peer), device_id_type=MESH)

    loads = [
        pltpu.make_async_copy(first_hbm.at[0], first_v, load_sem.at[0]),
        pltpu.make_async_copy(second_hbm.at[0], second_v, load_sem.at[1]),
        pltpu.make_async_copy(win_hbm.at[0, 0], wgu.at[:, pl.ds(0, HID)], load_sem.at[2]),
        pltpu.make_async_copy(win_hbm.at[0, 1], wgu.at[:, pl.ds(HID, HID)], load_sem.at[3]),
        pltpu.make_async_copy(wout_hbm.at[0], wout, load_sem.at[4]),
    ]
    early = [
        pltpu.make_async_copy(routes_hbm, routes_v, load_sem.at[5]),
        pltpu.make_async_copy(gates_hbm, gates_v, load_sem.at[6]),
        pltpu.make_async_copy(tok_hbm, tok_v, load_sem.at[7]),
        pltpu.make_async_copy(grad_hbm, grad_v, load_sem.at[8]),
    ]
    for load in early + loads:
        load.start()
    for load in early:
        load.wait()
    prepare(
        previous_ref,
        routes_v,
        gates_v,
        tok_v,
        grad_v,
        send_ref,
        main_ref,
        over_ref,
        code_x,
        gate_x,
    )
    pl.semaphore_wait(barrier, NE - 1 + 4)

    def rows16(j):
        return pl.ds(pl.multiple_of(j * MAIN, MAIN), MAIN)

    def remote(src, dst, ss, rs, who):
        return pltpu.make_async_remote_copy(
            src_ref=src, dst_ref=dst, send_sem=ss, recv_sem=rs, device_id=who, device_id_type=MESH
        )

    def disp(k):
        to = target(k)
        return remote(
            send_ref.at[rows16(to)], g.at[d, rows16(e)], disp_ss.at[k], disp_rs.at[k], (to, d)
        )

    def raw(k):
        to = target(k)
        return remote(raw_s.at[to], raw_r.at[e], raw_ss.at[k], raw_rs.at[k], (to, d))

    def wg(k):
        to = target(k)
        return remote(wg_s.at[to], wg_r.at[e], wg_ss.at[k], wg_rs.at[k], (to, d))

    def back(k):
        to = target(k)
        return remote(back_s.at[to], back_ref.at[e], back_ss.at[k], back_rs.at[k], (to, d))

    def ret(k):
        to = target(k)
        return remote(
            ret_s.at[rows16(to)], ret_ref.at[rows16(e)], ret_ss.at[k], ret_rs.at[k], (to, d)
        )

    loop(lambda k: disp(k).start(), 1, LEAD * NX)
    own = [
        pltpu.make_async_copy(send_ref.at[rows16(e)], g.at[d, rows16(e)], own_sem.at[0]),
        pltpu.make_async_copy(raw_s.at[e], raw_r.at[e], own_sem.at[1]),
        pltpu.make_async_copy(wg_s.at[e], wg_r.at[e], own_sem.at[2]),
        pltpu.make_async_copy(back_s.at[e], back_ref.at[e], own_sem.at[3]),
        pltpu.make_async_copy(ret_s.at[rows16(e)], ret_ref.at[rows16(e)], own_sem.at[4]),
    ]
    own[0].start()

    loads[0].wait()
    loads[1].wait()

    def cut(j):
        cols = pl.ds(pl.multiple_of(j * LANE, LANE), LANE)
        raw_s[j, 0] = first_v[0:RAW, cols].astype(BF16)
        raw_s[j, 1] = second_v[0:RAW, cols].astype(BF16)

    loop(cut, 0)
    r, q = iota((ROWS, ROWS), 0), iota((ROWS, ROWS), 1)
    spot = (r % EXTRA) // OVER * MAIN + r // EXTRA * OVER + r % OVER
    sel[...] = jnp.where(q == spot, 1.0, 0.0).astype(BF16)

    def block(i):
        return pl.ds(pl.multiple_of(lax.rem(z + NZ - dz_of(i), NZ) * BLOCK, BLOCK), BLOCK)

    def near(way, hop, i):
        step = 1 if way == 0 else -1
        held = g.at[y_of(-step * hop), block(i)]
        n = (way * 2 + hop) * NZ + i
        return remote(held, held, near_ss.at[n], near_rs.at[n], (e, y_of(step)))

    def side(back_by, i):
        held = g.at[y_of(-back_by), block(i)]
        n = (back_by % NY) * NZ + i
        return remote(held, held, sib_ss.at[n], sib_rs.at[n], (e, sib))

    def from_near(i):
        near(0, 0, i).wait_recv()
        if i % 2 == 0:
            near(0, 1, i).start()
        side(1, i).start()
        near(1, 0, i).wait_recv()
        if i % 2 == 1:
            near(1, 1, i).start()
        side(3, i).start()

    def from_far(i):
        near(i % 2, 1, i).wait_recv()
        side(2, i).start()

    sent = 1
    for i in range(NZ + 2):
        if i < NZ:
            if i == 0:
                own[0].wait()
            loop(lambda k: disp(k).wait_recv(), max(1, i * NX), (i + 1) * NX)
            near(0, 0, i).start()
            near(1, 0, i).start()
            side(0, i).start()
            if i + LEAD < NZ:
                loop(lambda k: disp(k).start(), (i + LEAD) * NX, (i + LEAD + 1) * NX)
        if 1 <= i <= NZ:
            from_near(i - 1)
        if i >= 2:
            from_far(i - 2)
        if i >= RAW_AT and sent < NE:
            more = min(NE, sent + RAW_N)
            loop(lambda k: raw(k).start(), sent, more)
            sent = more
    if sent < NE:
        loop(lambda k: raw(k).start(), sent, NE)
    own[1].start()
    for load in loads[2:]:
        load.wait()

    def part(j):
        return pl.ds(pl.multiple_of(j * FEAT, FEAT), FEAT)

    def lanes(j):
        return pl.ds(pl.multiple_of(j * LANE, LANE), LANE)

    def unpack(j):
        moved = dot(sel[...], g[j, :, 2 * FEAT : PACK]).astype(BF16)
        for k in range(4):
            xt[:, lanes(j * 4 + k)] = moved[k * EXTRA : (k + 1) * EXTRA]
            xg[:, lanes(j * 4 + k)] = moved[(k + 4) * EXTRA : (k + 5) * EXTRA]

    acc[...] = jnp.zeros_like(acc)
    agrad[...] = jnp.zeros_like(agrad)

    def forward(j):
        w = wgu[part(j), :]
        acc[0:ROWS] += dot(g[j, :, 0:FEAT], w)
        acc[ROWS:SLOTS] += dot(xt[:, part(j)], w)
        o = wout[:, part(j)]
        agrad[0:ROWS] += dot(g[j, :, FEAT : 2 * FEAT], o, ((1,), (1,)))
        agrad[ROWS:SLOTS] += dot(xg[:, part(j)], o, ((1,), (1,)))

    def origin(by, core):
        j = lax.rem(y + by, NY) * 2 + core
        unpack(j)
        forward(j)

    loop(lambda by: origin(by, c), 0, NY)
    for i in range(NZ):
        for b in (0, 1, 3):
            side(b, i).wait_recv()
    loop(lambda by: origin(by, 1 - c), NY - 1, NY + 2)
    for i in range(NZ):
        side(2, i).wait_recv()
    origin(2, 1 - c)

    def pointwise(j):
        rows = pl.ds(pl.multiple_of(j * EXTRA, EXTRA), EXTRA)
        gate, up, ag = acc[rows, 0:HID], acc[rows, HID : 2 * HID], agrad[rows]
        sig = jax.nn.sigmoid(gate)
        silu = gate * sig
        act[rows] = silu * up
        gu[rows, 0:HID] = (ag * up * sig * (1.0 + gate * (1.0 - sig))).astype(BF16)
        gu[rows, HID : 2 * HID] = (ag * silu).astype(BF16)

    loop(pointwise, 0, SLOTS // EXTRA)
    act_t[...] = act[...].T.astype(BF16)

    def outer(j):
        w = dot(act_t[:, 0:ROWS], g[j, :, FEAT : 2 * FEAT])
        w = w + dot(act_t[:, ROWS:SLOTS], xg[:, part(j)])
        for k in range(4):
            n = j * 4 + k
            piece = w[:, k * LANE : (k + 1) * LANE]
            wg_s[n, 0:RAW] = piece[0:RAW].astype(BF16)
            one, two = first_v[RAW:HID, lanes(n)], second_v[RAW:HID, lanes(n)]
            piece = piece[RAW:HID]
            wg_s[n, RAW:HID] = (beta_one * one + (1.0 - beta_one) * piece).astype(BF16)
            wg_s[n, HID:POST] = (beta_two * two + (1.0 - beta_two) * piece * piece).astype(BF16)

    outer(z)
    loop(lambda k: wg(k).start(), 1, NX)
    own[2].start()

    def outward(i):
        outer(lax.div(target(i * NX), NX))
        for dx in range(NX):
            wg(i * NX + dx).start()

    loop(outward, 1, NZ)

    def share(j):
        u[j] = dot(gu[...], wgu[part(j), :], ((1,), (1,))).astype(BF16)

    def to_sib(j):
        return remote(u.at[j * 2 + 1 - c], sib_r.at[j], sum_ss.at[j], sum_rs.at[j], (e, sib))

    def shares_out(j):
        share(j * 2 + 1 - c)
        to_sib(j).start()

    loop(shares_out, 0, NY)
    loop(lambda j: share(j * 2 + c), 0, NY)

    def to_y(o):
        return remote(
            pair.at[o], y_r.at[o], ysum_ss.at[o], ysum_rs.at[o], (e, lax.rem(y + o, NY) * 2 + c)
        )

    loop(lambda j: to_sib(j).wait_recv(), 0, NY)
    for o in (1, 3, 2, 0):
        ty = lax.rem(y + o, NY)
        pair[o] = (u[ty * 2 + c].astype(F32) + sib_r[ty].astype(F32)).astype(BF16)
        if o:
            to_y(o).start()

    own[1].wait()
    own[2].wait()
    loop(lambda k: raw(k).wait_recv())
    loop(lambda k: wg(k).wait_recv())

    def update(to):
        j = jnp.int32(0)
        for n in range(NE):
            j = j + jnp.where(next_ref[n] == to, previous_ref[n], 0)
        w = wg_r[j, 0:RAW].astype(F32)
        one, two = raw_r[j, 0].astype(F32), raw_r[j, 1].astype(F32)
        back_s[to, 0, 0:RAW] = (beta_one * one + (1.0 - beta_one) * w).astype(BF16)
        back_s[to, 1, 0:RAW] = (beta_two * two + (1.0 - beta_two) * w * w).astype(BF16)
        back_s[to, 0, RAW:HID] = wg_r[j, RAW:HID]
        back_s[to, 1, RAW:HID] = wg_r[j, HID:POST]

    def send_back(k):
        update(target(k))
        back(k).start()

    loop(send_back)
    update(e)
    own[3].start()

    for o in (1, 3, 2):
        to_y(o).wait_recv()

    def total(rows):
        value = pair[0, rows].astype(F32)
        for o in (1, 2, 3):
            value = value + y_r[o, rows].astype(F32)
        return value.astype(BF16)

    def add(j):
        rows = pl.ds(pl.multiple_of(j * EXTRA, EXTRA), EXTRA)
        ret_s[rows, 0:FEAT] = total(rows)

    loop(add, 0, ROWS // EXTRA)
    rest = total(pl.ds(ROWS, EXTRA))
    packed = jnp.zeros((ROWS, LANE), F32)
    for k in range(4):
        packed = packed + dot(
            sel[k * EXTRA : (k + 1) * EXTRA, :],
            rest[:, k * LANE : (k + 1) * LANE],
            ((0,), (0,)),
        )
    ret_s[:, FEAT:BACK] = packed.astype(BF16)
    loop(lambda k: ret(k).start())
    own[4].start()

    loop(lambda k: disp(k).wait_send())
    loop(lambda k: raw(k).wait_send())
    loop(lambda k: wg(k).wait_send())
    for i in range(NZ):
        near(0, 0, i).wait_send()
        near(1, 0, i).wait_send()
        near(i % 2, 1, i).wait_send()
        for b in range(NY):
            side(b, i).wait_send()
    loop(lambda j: to_sib(j).wait_send(), 0, NY)
    loop(lambda o: to_y(o).wait_send(), 1, NY)
    own[3].wait()
    loop(lambda k: back(k).wait())
    own[4].wait()
    loop(lambda k: ret(k).wait())


def finish_kernel(back_ref, ret_ref, main_ref, over_ref, tok_ref, first_ref, second_ref, step_ref):
    for k in range(4):
        cols = slice(k * LANE, (k + 1) * LANE)
        one, two = back_ref[k, 0].astype(F32), back_ref[k, 1].astype(F32)
        first_ref[0, :, cols] = one
        second_ref[0, :, cols] = two
        step_ref[0, :, cols] = (one / (jnp.sqrt(two) + epsilon)).astype(BF16)

    @pl.when(pl.program_id(0) == 0)
    def _():
        total = dot(main_ref[...], ret_ref[:, 0:FEAT], ((0,), (0,)))
        chunk = iota((ROWS, TOK), 0) % MAIN // OVER
        for k in range(4):
            cols = slice(k * LANE, (k + 1) * LANE)
            part = jnp.where(chunk == k, over_ref[...].astype(F32), 0.0).astype(BF16)
            more = dot(part, ret_ref[:, FEAT:BACK], ((0,), (0,)))
            tok_ref[:, cols] = (total[:, cols] + more).astype(BF16)


def per_device(
    tokens,
    out_grad,
    routes,
    gate_weights,
    previous_home,
    next_home,
    w_in,
    w_out,
    first_moment,
    second_moment,
):
    vmem = pl.BlockSpec(memory_space=pltpu.VMEM)
    smem = pl.BlockSpec(memory_space=pltpu.SMEM)
    anywhere = pl.BlockSpec(memory_space=pl.ANY)
    shape = jax.ShapeDtypeStruct
    dma = pltpu.SemaphoreType.DMA
    ret, back, place_main, place_over = pl.pallas_call(
        main_kernel,
        out_shape=(
            shape((ROWS, BACK), BF16),
            shape((NE, 2, HID, LANE), BF16),
            shape((ROWS, TOK), BF16),
            shape((ROWS, TOK), BF16),
        ),
        in_specs=[smem, smem] + [anywhere] * 8,
        out_specs=(vmem,) * 4,
        scratch_shapes=[
            pltpu.VMEM((TOP, TOK), jnp.int32),
            pltpu.VMEM((TOP, TOK), F32),
            pltpu.VMEM((TOK, FEAT), BF16),
            pltpu.VMEM((TOK, FEAT), BF16),
            pltpu.VMEM((ROWS, PACK), BF16),
            pltpu.VMEM((ROWS, TOK), F32),
            pltpu.VMEM((ROWS, TOK), F32),
            pltpu.VMEM((ND, ROWS, PACK), BF16),
            pltpu.VMEM((HID, WIDTH), F32),
            pltpu.VMEM((HID, WIDTH), F32),
            pltpu.VMEM((WIDTH, 2 * HID), BF16),
            pltpu.VMEM((HID, WIDTH), BF16),
            pltpu.VMEM((NE, 2, RAW, LANE), BF16),
            pltpu.VMEM((NE, 2, RAW, LANE), BF16),
            pltpu.VMEM((NE, POST, LANE), BF16),
            pltpu.VMEM((NE, POST, LANE), BF16),
            pltpu.VMEM((NE, 2, HID, LANE), BF16),
            pltpu.VMEM((ND, SLOTS, FEAT), BF16),
            pltpu.VMEM((NY, SLOTS, FEAT), BF16),
            pltpu.VMEM((NY, SLOTS, FEAT), BF16),
            pltpu.VMEM((NY, SLOTS, FEAT), BF16),
            pltpu.VMEM((EXTRA, WIDTH), BF16),
            pltpu.VMEM((EXTRA, WIDTH), BF16),
            pltpu.VMEM((SLOTS, 2 * HID), F32),
            pltpu.VMEM((SLOTS, HID), F32),
            pltpu.VMEM((SLOTS, HID), F32),
            pltpu.VMEM((HID, SLOTS), BF16),
            pltpu.VMEM((SLOTS, 2 * HID), BF16),
            pltpu.VMEM((ROWS, BACK), BF16),
            pltpu.VMEM((ROWS, ROWS), BF16),
            dma((9,)),
            dma((5,)),
        ]
        + [dma((NE,))] * 14
        + [dma((NY,))] * 4,
        compiler_params=pltpu.CompilerParams(
            collective_id=0, has_side_effects=True, vmem_limit_bytes=VMEM_LIMIT
        ),
        cost_estimate=pl.CostEstimate(
            flops=4 * 10**9, bytes_accessed=16 << 20, transcendentals=1 << 17
        ),
        name="exchange",
    )(
        previous_home,
        next_home,
        routes.T,
        gate_weights.T,
        tokens,
        out_grad,
        first_moment,
        second_moment,
        w_in,
        w_out,
    )

    steps = 8
    span = WIDTH // steps
    whole = lambda s: pl.BlockSpec(s, lambda i: (0,) * len(s))
    wide = pl.BlockSpec((1, HID, span), lambda i: (0, 0, i))
    return pl.pallas_call(
        finish_kernel,
        grid=(steps,),
        out_shape=(
            shape((TOK, FEAT), BF16),
            shape((1, HID, WIDTH), F32),
            shape((1, HID, WIDTH), F32),
            shape((1, HID, WIDTH), BF16),
        ),
        in_specs=[
            pl.BlockSpec((NE // steps, 2, HID, LANE), lambda i: (i, 0, 0, 0)),
            whole((ROWS, BACK)),
            whole((ROWS, TOK)),
            whole((ROWS, TOK)),
        ],
        out_specs=(whole((TOK, FEAT)), wide, wide, wide),
        compiler_params=pltpu.CompilerParams(vmem_limit_bytes=VMEM_LIMIT),
        cost_estimate=pl.CostEstimate(
            flops=3 * 10**8, bytes_accessed=8 << 20, transcendentals=1 << 19
        ),
        name="finish",
    )(back, ret, place_main, place_over)


def solution(mesh):
    return jax.shard_map(
        per_device,
        mesh=mesh,
        in_specs=(
            P("expert", "dp"),
            P("expert", "dp"),
            P("expert", None),
            P("expert", None),
            P(),
            P(),
            P("expert", None, None, "dp"),
            P("expert", "dp", None),
            P("expert", "dp", None),
            P("expert", "dp", None),
        ),
        out_specs=(
            P("expert", "dp"),
            P("expert", "dp", None),
            P("expert", "dp", None),
            P("expert", "dp", None),
        ),
        check_vma=False,
    )
```

```python
import functools

import jax
import jax.numpy as jnp
from jax import lax
from jax.experimental import pallas as pl
from jax.experimental.pallas import tpu as pltpu
from jax.sharding import PartitionSpec as P

beta_one = 0.9
beta_two = 0.95
epsilon = 1e-08

NE = 32
NZ, NX = 8, 4
ND = 8
NY = 4
TOK = 128
TOP = 4
MAIN = 16
OVER = 2
LANE = 128
FEAT = 512
WIDTH = 4096
HID = 128
ROWS = NE * MAIN
EXTRA = NE * OVER
SLOTS = ROWS + EXTRA
PACK = 2 * FEAT + LANE
BACK = FEAT + LANE
BLOCK = NX * MAIN
HALF = HID // 2
RAW = 48
POST = 2 * HALF - RAW
RAW_AT = 3
RAW_N = 8
LEAD = 5
F32 = jnp.float32
BF16 = jnp.bfloat16
MESH = pl.DeviceIdType.MESH
VMEM_LIMIT = 60 << 20


def iota(shape, dim):
    return lax.broadcasted_iota(jnp.int32, shape, dim)


def dot(a, b, dims=((1,), (0,))):
    return lax.dot_general(a, b, (dims, ((), ())), preferred_element_type=F32)


def prepare(
    home_ref, routes_ref, gates_ref, tok_ref, grad_ref, send_ref, main_ref, over_ref, code_x, gate_x
):
    routes = routes_ref[...]
    target = jnp.zeros_like(routes)
    for e in range(NE):
        target = jnp.where(routes == e, home_ref[e], target)
    dest = iota((NE, TOK), 0)
    chosen = jnp.zeros((NE, TOK), F32)
    gate = jnp.zeros((NE, TOK), F32)
    for k in range(TOP):
        same = target[k : k + 1, :] == dest
        chosen = jnp.where(same, 1.0, chosen)
        gate = jnp.where(same, gates_ref[k : k + 1, :], gate)
    earlier = jnp.where(iota((TOK, TOK), 0) < iota((TOK, TOK), 1), 1.0, 0.0).astype(BF16)
    count = dot(chosen.astype(BF16), earlier)
    code = jnp.where(chosen > 0.5, count, -1.0)
    for j in range(NE):
        rows = pl.ds(j * MAIN, MAIN)
        code_x[rows, :] = jnp.broadcast_to(code[j : j + 1, :], (MAIN, TOK))
        gate_x[rows, :] = jnp.broadcast_to(gate[j : j + 1, :], (MAIN, TOK))
    code = code_x[...]
    gate = gate_x[...]
    within = iota((ROWS, TOK), 0) % MAIN
    hit = code == within.astype(F32)
    place = jnp.where(hit, 1.0, 0.0).astype(BF16)
    scale = jnp.sum(jnp.where(hit, gate, 0.0), axis=1, keepdims=True)
    main_ref[...] = place
    send_ref[:, 0:FEAT] = dot(place, tok_ref[...]).astype(BF16)
    send_ref[:, FEAT : 2 * FEAT] = (dot(place, grad_ref[...]) * scale).astype(BF16)
    hit = code == (MAIN + within % OVER).astype(F32)
    scale = jnp.sum(jnp.where(hit, gate, 0.0), axis=1, keepdims=True)
    over_ref[...] = jnp.where(hit, 1.0, 0.0).astype(BF16)
    chunk = within // OVER
    packed = jnp.zeros((ROWS, LANE), F32)
    for c in range(8):
        part = jnp.where(hit & (chunk == c), 1.0, 0.0).astype(BF16)
        held = tok_ref if c < 4 else grad_ref
        packed = packed + dot(part, held[:, (c % 4) * LANE : (c % 4 + 1) * LANE])
    packed = jnp.where(chunk >= 4, packed * scale, packed)
    send_ref[:, 2 * FEAT : PACK] = packed.astype(BF16)


def main_kernel(
    previous_ref,
    next_ref,
    routes_hbm,
    gates_hbm,
    tok_hbm,
    grad_hbm,
    first_hbm,
    second_hbm,
    win_hbm,
    wout_hbm,
    ret_ref,
    back_ref,
    main_ref,
    over_ref,
    routes_v,
    gates_v,
    tok_v,
    grad_v,
    send_ref,
    code_x,
    gate_x,
    g,
    first_v,
    second_v,
    wgu,
    wout,
    raw_s,
    raw_r,
    wg_s,
    wg_r0,
    wg_r1,
    back_s,
    u,
    sib_r,
    pair,
    y_r,
    xt,
    xg,
    acc,
    agrad,
    act,
    act_t,
    gu,
    ret_s,
    sel,
    load_sem,
    own_sem,
    disp_ss,
    disp_rs,
    raw_ss,
    raw_rs,
    wg_ss,
    wg_rs,
    back_ss,
    back_rs,
    ret_ss,
    ret_rs,
    near_ss,
    near_rs,
    sib_ss,
    sib_rs,
    sum_ss,
    sum_rs,
    ysum_ss,
    ysum_rs,
):
    e = lax.axis_index("expert")
    d = lax.axis_index("dp")
    z, x = lax.div(e, NX), lax.rem(e, NX)
    y, c = lax.div(d, 2), lax.rem(d, 2)
    sib = y * 2 + 1 - c
    wg_r = (wg_r0, wg_r1)

    def dz_of(i):
        odd = i % 2
        return odd * ((i + 1) // 2) + (1 - odd) * ((NZ - i // 2) % NZ)

    def target(k):
        i, dx = lax.div(k, NX), lax.rem(k, NX)
        odd = lax.rem(i, 2)
        dz = odd * lax.div(i + 1, 2) + (1 - odd) * lax.rem(NZ - lax.div(i, 2), NZ)
        return lax.rem(z + dz, NZ) * NX + lax.rem(x + dx, NX)

    def y_of(step):
        return lax.rem(y + step + NY, NY) * 2 + c

    def loop(body, lower=1, upper=NE):
        def step(k, carry):
            body(k)
            return carry

        lax.fori_loop(lower, upper, step, 0)

    barrier = pltpu.get_barrier_semaphore()

    def greet(k):
        pl.semaphore_signal(barrier, inc=1, device_id=(target(k), d), device_id_type=MESH)

    loop(greet)
    for peer in (y_of(1), y_of(2), y_of(3), sib):
        pl.semaphore_signal(barrier, inc=1, device_id=(e, peer), device_id_type=MESH)

    loads = [
        pltpu.make_async_copy(first_hbm.at[0], first_v, load_sem.at[0]),
        pltpu.make_async_copy(second_hbm.at[0], second_v, load_sem.at[1]),
        pltpu.make_async_copy(win_hbm.at[0, 0], wgu.at[:, pl.ds(0, HID)], load_sem.at[2]),
        pltpu.make_async_copy(win_hbm.at[0, 1], wgu.at[:, pl.ds(HID, HID)], load_sem.at[3]),
        pltpu.make_async_copy(wout_hbm.at[0], wout, load_sem.at[4]),
    ]
    early = [
        pltpu.make_async_copy(routes_hbm, routes_v, load_sem.at[5]),
        pltpu.make_async_copy(gates_hbm, gates_v, load_sem.at[6]),
        pltpu.make_async_copy(tok_hbm, tok_v, load_sem.at[7]),
        pltpu.make_async_copy(grad_hbm, grad_v, load_sem.at[8]),
    ]
    for load in early + loads:
        load.start()
    for load in early:
        load.wait()
    prepare(
        previous_ref,
        routes_v,
        gates_v,
        tok_v,
        grad_v,
        send_ref,
        main_ref,
        over_ref,
        code_x,
        gate_x,
    )
    pl.semaphore_wait(barrier, NE - 1 + 4)

    def rows16(j):
        return pl.ds(pl.multiple_of(j * MAIN, MAIN), MAIN)

    def remote(src, dst, ss, rs, who):
        return pltpu.make_async_remote_copy(
            src_ref=src, dst_ref=dst, send_sem=ss, recv_sem=rs, device_id=who, device_id_type=MESH
        )

    def disp(k):
        to = target(k)
        return remote(
            send_ref.at[rows16(to)], g.at[d, rows16(e)], disp_ss.at[k], disp_rs.at[k], (to, d)
        )

    def raw(k):
        to = target(k)
        return remote(raw_s.at[to], raw_r.at[e], raw_ss.at[k], raw_rs.at[k], (to, d))

    def wg(h, k):
        to, n = target(k), h * NE + k
        return remote(wg_s.at[h, to], wg_r[h].at[e], wg_ss.at[n], wg_rs.at[n], (to, d))

    def back(h, k):
        to, n = target(k), h * NE + k
        return remote(back_s.at[h, to], back_ref.at[h, e], back_ss.at[n], back_rs.at[n], (to, d))

    def ret(k):
        to = target(k)
        return remote(
            ret_s.at[rows16(to)], ret_ref.at[rows16(e)], ret_ss.at[k], ret_rs.at[k], (to, d)
        )

    loop(lambda k: disp(k).start(), 1, LEAD * NX)
    own = [
        pltpu.make_async_copy(send_ref.at[rows16(e)], g.at[d, rows16(e)], own_sem.at[0]),
        pltpu.make_async_copy(raw_s.at[e], raw_r.at[e], own_sem.at[1]),
        pltpu.make_async_copy(wg_s.at[0, e], wg_r[0].at[e], own_sem.at[2]),
        pltpu.make_async_copy(back_s.at[0, e], back_ref.at[0, e], own_sem.at[3]),
        pltpu.make_async_copy(ret_s.at[rows16(e)], ret_ref.at[rows16(e)], own_sem.at[4]),
        pltpu.make_async_copy(wg_s.at[1, e], wg_r[1].at[e], own_sem.at[5]),
        pltpu.make_async_copy(back_s.at[1, e], back_ref.at[1, e], own_sem.at[6]),
    ]
    own[0].start()

    loads[0].wait()
    loads[1].wait()

    def cut(j):
        cols = pl.ds(pl.multiple_of(j * LANE, LANE), LANE)
        for h in range(2):
            rows = slice(h * HALF, h * HALF + RAW)
            raw_s[j, 0, h] = first_v[rows, cols].astype(BF16)
            raw_s[j, 1, h] = second_v[rows, cols].astype(BF16)

    loop(cut, 0)
    r, q = iota((ROWS, ROWS), 0), iota((ROWS, ROWS), 1)
    spot = (r % EXTRA) // OVER * MAIN + r // EXTRA * OVER + r % OVER
    sel[...] = jnp.where(q == spot, 1.0, 0.0).astype(BF16)

    def block(i):
        return pl.ds(pl.multiple_of(lax.rem(z + NZ - dz_of(i), NZ) * BLOCK, BLOCK), BLOCK)

    def near(way, hop, i):
        step = 1 if way == 0 else -1
        held = g.at[y_of(-step * hop), block(i)]
        n = (way * 2 + hop) * NZ + i
        return remote(held, held, near_ss.at[n], near_rs.at[n], (e, y_of(step)))

    def side(back_by, i):
        held = g.at[y_of(-back_by), block(i)]
        n = (back_by % NY) * NZ + i
        return remote(held, held, sib_ss.at[n], sib_rs.at[n], (e, sib))

    def from_near(i):
        near(0, 0, i).wait_recv()
        if i % 2 == 0:
            near(0, 1, i).start()
        side(1, i).start()
        near(1, 0, i).wait_recv()
        if i % 2 == 1:
            near(1, 1, i).start()
        side(3, i).start()

    def from_far(i):
        near(i % 2, 1, i).wait_recv()
        side(2, i).start()

    sent = 1
    for i in range(NZ + 2):
        if i < NZ:
            if i == 0:
                own[0].wait()
            loop(lambda k: disp(k).wait_recv(), max(1, i * NX), (i + 1) * NX)
            near(0, 0, i).start()
            near(1, 0, i).start()
            side(0, i).start()
            if i + LEAD < NZ:
                loop(lambda k: disp(k).start(), (i + LEAD) * NX, (i + LEAD + 1) * NX)
        if 1 <= i <= NZ:
            from_near(i - 1)
        if i >= 2:
            from_far(i - 2)
        if i >= RAW_AT and sent < NE:
            more = min(NE, sent + RAW_N)
            loop(lambda k: raw(k).start(), sent, more)
            sent = more
    if sent < NE:
        loop(lambda k: raw(k).start(), sent, NE)
    own[1].start()
    for load in loads[2:]:
        load.wait()

    def part(j):
        return pl.ds(pl.multiple_of(j * FEAT, FEAT), FEAT)

    def lanes(j):
        return pl.ds(pl.multiple_of(j * LANE, LANE), LANE)

    def unpack(j):
        moved = dot(sel[...], g[j, :, 2 * FEAT : PACK]).astype(BF16)
        for k in range(4):
            xt[:, lanes(j * 4 + k)] = moved[k * EXTRA : (k + 1) * EXTRA]
            xg[:, lanes(j * 4 + k)] = moved[(k + 4) * EXTRA : (k + 5) * EXTRA]

    acc[...] = jnp.zeros_like(acc)
    agrad[...] = jnp.zeros_like(agrad)

    def forward(j):
        w = wgu[part(j), :]
        acc[0:ROWS] += dot(g[j, :, 0:FEAT], w)
        acc[ROWS:SLOTS] += dot(xt[:, part(j)], w)
        o = wout[:, part(j)]
        agrad[0:ROWS] += dot(g[j, :, FEAT : 2 * FEAT], o, ((1,), (1,)))
        agrad[ROWS:SLOTS] += dot(xg[:, part(j)], o, ((1,), (1,)))

    def origin(by, core):
        j = lax.rem(y + by, NY) * 2 + core
        unpack(j)
        forward(j)

    loop(lambda by: origin(by, c), 0, NY)
    for i in range(NZ):
        for b in (0, 1, 3):
            side(b, i).wait_recv()
    loop(lambda by: origin(by, 1 - c), NY - 1, NY + 2)
    for i in range(NZ):
        side(2, i).wait_recv()
    origin(2, 1 - c)

    def pointwise(j):
        rows = pl.ds(pl.multiple_of(j * EXTRA, EXTRA), EXTRA)
        gate, up, ag = acc[rows, 0:HID], acc[rows, HID : 2 * HID], agrad[rows]
        sig = jax.nn.sigmoid(gate)
        silu = gate * sig
        act[rows] = silu * up
        gu[rows, 0:HID] = (ag * up * sig * (1.0 + gate * (1.0 - sig))).astype(BF16)
        gu[rows, HID : 2 * HID] = (ag * silu).astype(BF16)

    loop(pointwise, 0, SLOTS // EXTRA)
    act_t[...] = act[...].T.astype(BF16)

    def outer(j):
        w = dot(act_t[:, 0:ROWS], g[j, :, FEAT : 2 * FEAT])
        w = w + dot(act_t[:, ROWS:SLOTS], xg[:, part(j)])
        for k in range(4):
            n = j * 4 + k
            piece = w[:, k * LANE : (k + 1) * LANE]
            for h in range(2):
                wg_s[h, n, 0:RAW] = piece[h * HALF : h * HALF + RAW].astype(BF16)
                rows = slice(h * HALF + RAW, (h + 1) * HALF)
                one, two, p = first_v[rows, lanes(n)], second_v[rows, lanes(n)], piece[rows]
                one = beta_one * one + (1.0 - beta_one) * p
                two = beta_two * two + (1.0 - beta_two) * p * p
                wg_s[h, n, RAW:HALF] = one.astype(BF16)
                wg_s[h, n, HALF:POST] = two.astype(BF16)

    outer(z)
    loop(lambda k: wg(0, k).start(), 1, NX)
    own[2].start()

    def outward(i):
        outer(lax.div(target(i * NX), NX))
        for dx in range(NX):
            wg(0, i * NX + dx).start()

    loop(outward, 1, NZ)
    loop(lambda k: wg(1, k).start())
    own[5].start()

    def share(j):
        u[j] = dot(gu[...], wgu[part(j), :], ((1,), (1,))).astype(BF16)

    def to_sib(j):
        return remote(u.at[j * 2 + 1 - c], sib_r.at[j], sum_ss.at[j], sum_rs.at[j], (e, sib))

    def shares_out(j):
        share(j * 2 + 1 - c)
        to_sib(j).start()

    loop(shares_out, 0, NY)
    loop(lambda j: share(j * 2 + c), 0, NY)

    def to_y(o):
        return remote(
            pair.at[o], y_r.at[o], ysum_ss.at[o], ysum_rs.at[o], (e, lax.rem(y + o, NY) * 2 + c)
        )

    loop(lambda j: to_sib(j).wait_recv(), 0, NY)
    for o in (1, 3, 2, 0):
        ty = lax.rem(y + o, NY)
        pair[o] = (u[ty * 2 + c].astype(F32) + sib_r[ty].astype(F32)).astype(BF16)
        if o:
            to_y(o).start()

    own[1].wait()
    loop(lambda k: raw(k).wait_recv())

    def update(h, to):
        j = jnp.int32(0)
        for n in range(NE):
            j = j + jnp.where(next_ref[n] == to, previous_ref[n], 0)
        w = wg_r[h][j, 0:RAW].astype(F32)
        one, two = raw_r[j, 0, h].astype(F32), raw_r[j, 1, h].astype(F32)
        one = beta_one * one + (1.0 - beta_one) * w
        two = beta_two * two + (1.0 - beta_two) * w * w
        back_s[h, to, 0, 0:RAW] = one.astype(BF16)
        back_s[h, to, 1, 0:RAW] = two.astype(BF16)
        back_s[h, to, 0, RAW:HALF] = wg_r[h][j, RAW:HALF]
        back_s[h, to, 1, RAW:HALF] = wg_r[h][j, HALF:POST]

    for h in range(2):
        own[2 + 3 * h].wait()
        loop(lambda k: wg(h, k).wait_recv())

        def send_back(k):
            update(h, target(k))
            back(h, k).start()

        loop(send_back)
        update(h, e)
        own[3 + 3 * h].start()

    for o in (1, 3, 2):
        to_y(o).wait_recv()

    def total(rows):
        value = pair[0, rows].astype(F32)
        for o in (1, 2, 3):
            value = value + y_r[o, rows].astype(F32)
        return value.astype(BF16)

    def add(j):
        rows = pl.ds(pl.multiple_of(j * EXTRA, EXTRA), EXTRA)
        ret_s[rows, 0:FEAT] = total(rows)

    loop(add, 0, ROWS // EXTRA)
    rest = total(pl.ds(ROWS, EXTRA))
    packed = jnp.zeros((ROWS, LANE), F32)
    for k in range(4):
        packed = packed + dot(
            sel[k * EXTRA : (k + 1) * EXTRA, :],
            rest[:, k * LANE : (k + 1) * LANE],
            ((0,), (0,)),
        )
    ret_s[:, FEAT:BACK] = packed.astype(BF16)
    loop(lambda k: ret(k).start())
    own[4].start()

    loop(lambda k: disp(k).wait_send())
    loop(lambda k: raw(k).wait_send())
    for h in range(2):
        loop(lambda k: wg(h, k).wait_send())
    for i in range(NZ):
        near(0, 0, i).wait_send()
        near(1, 0, i).wait_send()
        near(i % 2, 1, i).wait_send()
        for b in range(NY):
            side(b, i).wait_send()
    loop(lambda j: to_sib(j).wait_send(), 0, NY)
    loop(lambda o: to_y(o).wait_send(), 1, NY)
    for h in range(2):
        own[3 + 3 * h].wait()
        loop(lambda k: back(h, k).wait())
    own[4].wait()
    loop(lambda k: ret(k).wait())


def finish_kernel(back_ref, ret_ref, main_ref, over_ref, tok_ref, first_ref, second_ref, step_ref):
    for h in range(2):
        rows = slice(h * HALF, (h + 1) * HALF)
        for k in range(4):
            cols = slice(k * LANE, (k + 1) * LANE)
            one, two = back_ref[h, k, 0].astype(F32), back_ref[h, k, 1].astype(F32)
            first_ref[0, rows, cols] = one
            second_ref[0, rows, cols] = two
            step_ref[0, rows, cols] = (one / (jnp.sqrt(two) + epsilon)).astype(BF16)

    @pl.when(pl.program_id(0) == 0)
    def _():
        total = dot(main_ref[...], ret_ref[:, 0:FEAT], ((0,), (0,)))
        chunk = iota((ROWS, TOK), 0) % MAIN // OVER
        for k in range(4):
            cols = slice(k * LANE, (k + 1) * LANE)
            part = jnp.where(chunk == k, over_ref[...].astype(F32), 0.0).astype(BF16)
            more = dot(part, ret_ref[:, FEAT:BACK], ((0,), (0,)))
            tok_ref[:, cols] = (total[:, cols] + more).astype(BF16)


def per_device(
    tokens,
    out_grad,
    routes,
    gate_weights,
    previous_home,
    next_home,
    w_in,
    w_out,
    first_moment,
    second_moment,
):
    vmem = pl.BlockSpec(memory_space=pltpu.VMEM)
    smem = pl.BlockSpec(memory_space=pltpu.SMEM)
    anywhere = pl.BlockSpec(memory_space=pl.ANY)
    shape = jax.ShapeDtypeStruct
    dma = pltpu.SemaphoreType.DMA
    ret, back, place_main, place_over = pl.pallas_call(
        main_kernel,
        out_shape=(
            shape((ROWS, BACK), BF16),
            shape((2, NE, 2, HALF, LANE), BF16),
            shape((ROWS, TOK), BF16),
            shape((ROWS, TOK), BF16),
        ),
        in_specs=[smem, smem] + [anywhere] * 8,
        out_specs=(vmem,) * 4,
        scratch_shapes=[
            pltpu.VMEM((TOP, TOK), jnp.int32),
            pltpu.VMEM((TOP, TOK), F32),
            pltpu.VMEM((TOK, FEAT), BF16),
            pltpu.VMEM((TOK, FEAT), BF16),
            pltpu.VMEM((ROWS, PACK), BF16),
            pltpu.VMEM((ROWS, TOK), F32),
            pltpu.VMEM((ROWS, TOK), F32),
            pltpu.VMEM((ND, ROWS, PACK), BF16),
            pltpu.VMEM((HID, WIDTH), F32),
            pltpu.VMEM((HID, WIDTH), F32),
            pltpu.VMEM((WIDTH, 2 * HID), BF16),
            pltpu.VMEM((HID, WIDTH), BF16),
            pltpu.VMEM((NE, 2, 2, RAW, LANE), BF16),
            pltpu.VMEM((NE, 2, 2, RAW, LANE), BF16),
            pltpu.VMEM((2, NE, POST, LANE), BF16),
            pltpu.VMEM((NE, POST, LANE), BF16),
            pltpu.VMEM((NE, POST, LANE), BF16),
            pltpu.VMEM((2, NE, 2, HALF, LANE), BF16),
            pltpu.VMEM((ND, SLOTS, FEAT), BF16),
            pltpu.VMEM((NY, SLOTS, FEAT), BF16),
            pltpu.VMEM((NY, SLOTS, FEAT), BF16),
            pltpu.VMEM((NY, SLOTS, FEAT), BF16),
            pltpu.VMEM((EXTRA, WIDTH), BF16),
            pltpu.VMEM((EXTRA, WIDTH), BF16),
            pltpu.VMEM((SLOTS, 2 * HID), F32),
            pltpu.VMEM((SLOTS, HID), F32),
            pltpu.VMEM((SLOTS, HID), F32),
            pltpu.VMEM((HID, SLOTS), BF16),
            pltpu.VMEM((SLOTS, 2 * HID), BF16),
            pltpu.VMEM((ROWS, BACK), BF16),
            pltpu.VMEM((ROWS, ROWS), BF16),
            dma((9,)),
            dma((7,)),
        ]
        + [dma((NE,))] * 4
        + [dma((2 * NE,))] * 4
        + [dma((NE,))] * 6
        + [dma((NY,))] * 4,
        compiler_params=pltpu.CompilerParams(
            collective_id=0, has_side_effects=True, vmem_limit_bytes=VMEM_LIMIT
        ),
        cost_estimate=pl.CostEstimate(
            flops=4 * 10**9, bytes_accessed=16 << 20, transcendentals=1 << 17
        ),
        name="exchange",
    )(
        previous_home,
        next_home,
        routes.T,
        gate_weights.T,
        tokens,
        out_grad,
        first_moment,
        second_moment,
        w_in,
        w_out,
    )

    steps = 8
    span = WIDTH // steps
    whole = lambda s: pl.BlockSpec(s, lambda i: (0,) * len(s))
    wide = pl.BlockSpec((1, HID, span), lambda i: (0, 0, i))
    return pl.pallas_call(
        finish_kernel,
        grid=(steps,),
        out_shape=(
            shape((TOK, FEAT), BF16),
            shape((1, HID, WIDTH), F32),
            shape((1, HID, WIDTH), F32),
            shape((1, HID, WIDTH), BF16),
        ),
        in_specs=[
            pl.BlockSpec((2, NE // steps, 2, HALF, LANE), lambda i: (0, i, 0, 0, 0)),
            whole((ROWS, BACK)),
            whole((ROWS, TOK)),
            whole((ROWS, TOK)),
        ],
        out_specs=(whole((TOK, FEAT)), wide, wide, wide),
        compiler_params=pltpu.CompilerParams(vmem_limit_bytes=VMEM_LIMIT),
        cost_estimate=pl.CostEstimate(
            flops=3 * 10**8, bytes_accessed=8 << 20, transcendentals=1 << 19
        ),
        name="finish",
    )(back, ret, place_main, place_over)


def solution(mesh):
    return jax.shard_map(
        per_device,
        mesh=mesh,
        in_specs=(
            P("expert", "dp"),
            P("expert", "dp"),
            P("expert", None),
            P("expert", None),
            P(),
            P(),
            P("expert", None, None, "dp"),
            P("expert", "dp", None),
            P("expert", "dp", None),
            P("expert", "dp", None),
        ),
        out_specs=(
            P("expert", "dp"),
            P("expert", "dp", None),
            P("expert", "dp", None),
            P("expert", "dp", None),
        ),
        check_vma=False,
    )
```
